256 devices in a mesh: qa: 16 (over z_lo, y), qb: 16 (over z_hi, x, core).
Axes of the slice: x: 4, y: 4, z: 8 (z_hi: 2, z_lo: 4; z = z_hi * 4 + z_lo), core: 2. Of those that a mesh axis runs over, the one named last changes fastest.
Arguments:
- amplitudes: float32 [16, 16, 1048576], P('qa', 'qb'), may hold values from -6 to 6
- gates: float32 [3, 2, 128, 128], replicated, may hold values from -0.5 to 0.5
- cz_pairs: int32 [3, 20, 2], replicated, may hold values from 0 to 19, as said below
Outputs:
- final_state: float32 [16, 16, 1048576], P('qa', 'qb')
The draws below stay inside these ranges and needn't reach their ends.
Inputs may be any that keep to these rules, and one draw needn't show every extreme that they name: `cz_pairs`: in each layer the first qubits of the 20 pairs are all different, and the two qubits of a pair differ.
All inputs are finite; a program needn't handle non-finite values.
Results may differ from the reference program's by a relative error of at most 0.0001.
Values sent between devices are 32-bit elements; how exact they have to be, the bound alone decides.
No kernel may reach another device: no remote copies, remote signals or barrier semaphores. Data moves between devices by JAX's collectives and lax.ppermute only.
A program may use at most 64 MiB of HBM per device.

```python
import jax
import jax.numpy as jnp
from jax import lax

BLOCK = 128
LOCALQ = 20
LAYERS = 3
AMP_DEV = 1048576
N_QA = 16
N_QB = 16


def draw_cz_pairs(key, part):
    key = jax.random.fold_in(key, 7)
    key_list = jax.random.split(key, 2)
    layer_keys = jax.random.split(key_list[0], LAYERS)
    first_q = jax.vmap(lambda one_key: jax.random.permutation(one_key, LOCALQ))(layer_keys).astype(jnp.int32)
    offset = jax.random.randint(key_list[1], (LAYERS, LOCALQ), 1, LOCALQ).astype(jnp.int32)
    second_q = (first_q + offset) % LOCALQ
    return jnp.stack([first_q, second_q], -1).astype(jnp.int32)


def level_of(rng, dims, shards, smallest, top_value):
    factor_of, own = 1.0, jax.random.fold_in(rng, 6)
    for dim, parts in shards:
        steps = jnp.exp(jax.random.uniform(jax.random.fold_in(own, dim), (parts,), jnp.float32, smallest / len(shards), top_value / len(shards)))
        factor_of = factor_of * jnp.repeat(steps, dims[dim] // parts).reshape([-1 if axis == dim else 1 for axis in range(len(dims))])
    return factor_of


def noise(stream_key, shape, deviation, reach, shards=(), held_as=jnp.bfloat16):
    values = deviation * jax.random.normal(stream_key, shape, jnp.float32)
    if shards:
        values = values * level_of(stream_key, shape, shards, -0.22, 0.18)
    return jnp.clip(values, -reach, reach).astype(held_as)


def setup_inputs(seed: int = 0) -> dict:
    seeds = jax.random.split(jax.random.key(seed), 4)
    amplitudes = noise(seeds[0], (N_QA, N_QB, AMP_DEV), 1.0, 6.0, ((0, 16), (1, 16)), jnp.float32)
    gates = noise(seeds[1], (LAYERS, 2, BLOCK, BLOCK), BLOCK ** -0.5, 0.5, (), jnp.float32)
    cz_pairs = draw_cz_pairs(jax.random.fold_in(seeds[3], 71), 0)
    return {"amplitudes": amplitudes, "gates": gates, "cz_pairs": cz_pairs}


def cz_sign(positions, pair_list):
    parity = jnp.zeros(positions.shape, jnp.int32)
    for pair_idx in range(pair_list.shape[0]):
        first_bit = jnp.right_shift(positions, pair_list[pair_idx, 0]) & 1
        second_bit = jnp.right_shift(positions, pair_list[pair_idx, 1]) & 1
        parity = parity + first_bit * second_bit
    return 1.0 - 2.0 * (parity % 2).astype(jnp.float32)


def reference(amplitudes, gates, cz_pairs):
    total_amp = amplitudes.shape[2]
    side_len = gates.shape[-1]
    lead_rows = total_amp // (side_len * side_len)
    whole_state = amplitudes.reshape(N_QA * N_QB, lead_rows, side_len, side_len)
    positions = jnp.arange(total_amp, dtype=jnp.int32).reshape(lead_rows, side_len, side_len)
    for layer_idx in range(LAYERS):
        whole_state = jnp.einsum("nxyk,ik->nxyi", whole_state, gates[layer_idx, 0], precision=lax.Precision.HIGHEST)
        whole_state = jnp.einsum("nxky,ik->nxiy", whole_state, gates[layer_idx, 1], precision=lax.Precision.HIGHEST)
        whole_state = whole_state * cz_sign(positions, cz_pairs[layer_idx])[None]
        if layer_idx + 1 < LAYERS:
            seven_dims = whole_state.reshape(N_QA, N_QB, lead_rows, N_QA, side_len // N_QA, N_QB, side_len // N_QB)
            seven_dims = jnp.transpose(seven_dims, (3, 5, 2, 0, 4, 1, 6))
            whole_state = seven_dims.reshape(N_QA * N_QB, lead_rows, side_len, side_len)
    return whole_state.reshape(N_QA, N_QB, total_amp)
```

```python
import functools

import jax
import jax.numpy as jnp
from jax import lax
from jax.experimental import pallas as pl
from jax.experimental.pallas import tpu as pltpu
from jax.sharding import PartitionSpec as P

LAYERS = 3
SIDE = 128
ROWS_STEP = 1024
AXES = ("qa", "qb")
VMEM = 48 * 1024 * 1024


def split(value):
    high = value.astype(jnp.bfloat16)
    low = (value - high.astype(jnp.float32)).astype(jnp.bfloat16)
    return high, low


def gate_stack(gate):
    high, low = split(gate)
    return jnp.concatenate(
        [jnp.concatenate([high, high], 1), jnp.concatenate([low, low], 1)], 0
    )


def apply_rows(stack, value):
    high, low = split(value)
    both = jnp.dot(
        stack, jnp.concatenate([high, low], 0), preferred_element_type=jnp.float32
    )
    return both[:SIDE] + both[SIDE:]


def apply_lanes(stack, value):
    high, low = split(value)
    both = lax.dot_general(
        jnp.concatenate([high, low], 1),
        stack,
        (((1,), (1,)), ((), ())),
        preferred_element_type=jnp.float32,
    )
    return both[:, :SIDE] + both[:, SIDE:]


def sign_of(positions, pairs_ref, layer):
    parity = jnp.zeros(positions.shape, jnp.int32)
    for pair in range(pairs_ref.shape[1]):
        first = jnp.right_shift(positions, pairs_ref[layer, pair, 0])
        second = jnp.right_shift(positions, pairs_ref[layer, pair, 1])
        parity = parity ^ (first & second)
    return 1.0 - 2.0 * (parity & 1).astype(jnp.float32)


def fold_parity(value):
    for shift in (8, 4, 2, 1):
        value = value ^ jnp.right_shift(value, shift)
    return value & 1


def native_kernel(layer, slot, pairs_ref, masks_ref, gates_ref, in_ref, out_ref, stacks, table):
    step = pl.program_id(0)

    @pl.when(step == 0)
    def _():
        stacks[0] = gate_stack(gates_ref[layer, 0])
        stacks[1] = gate_stack(gates_ref[layer, 1])
        rows = lax.broadcasted_iota(jnp.int32, (SIDE, SIDE), 0)
        lanes = lax.broadcasted_iota(jnp.int32, (SIDE, SIDE), 1)
        table[...] = sign_of(rows * SIDE + lanes, pairs_ref, layer)

    low_bits = lax.broadcasted_iota(jnp.int32, (8, SIDE), 0) * SIDE + (
        lax.broadcasted_iota(jnp.int32, (8, SIDE), 1)
    )
    stack_z = stacks[0]
    stack_y = stacks[1]
    x_step = ROWS_STEP // SIDE
    for pair in range(x_step // 2):
        base = pair * 2 * SIDE
        value = apply_lanes(stack_z, in_ref[base : base + 2 * SIDE])
        value = apply_rows(
            stack_y, jnp.concatenate([value[:SIDE], value[SIDE:]], 1)
        )
        for half in range(2):
            mask = masks_ref[slot, step * x_step + pair * 2 + half]
            parity = fold_parity((low_bits & mask) ^ (jnp.right_shift(mask, 14) & 1))
            signs = [1.0 - 2.0 * parity.astype(jnp.float32)]
            for bit in range(4):
                flip = jnp.right_shift(mask, 10 + bit) & 1
                factor = 1.0 - 2.0 * flip.astype(jnp.float32)
                signs = signs + [sign * factor for sign in signs]
            sign = jnp.concatenate(signs, 0) * table[...]
            start = base + half * SIDE
            out_ref[start : start + SIDE] = (
                value[:, half * SIDE : (half + 1) * SIDE] * sign
            )


def native_layer(layer, slot, pairs, masks, gates, state):
    steps = state.shape[0] // ROWS_STEP
    return pl.pallas_call(
        functools.partial(native_kernel, layer, slot),
        grid=(steps,),
        in_specs=[
            pl.BlockSpec(memory_space=pltpu.SMEM),
            pl.BlockSpec(memory_space=pltpu.SMEM),
            pl.BlockSpec(memory_space=pltpu.VMEM),
            pl.BlockSpec((ROWS_STEP, SIDE), lambda i: (i, 0)),
        ],
        out_specs=pl.BlockSpec((ROWS_STEP, SIDE), lambda i: (i, 0)),
        out_shape=jax.ShapeDtypeStruct(state.shape, jnp.float32),
        scratch_shapes=[
            pltpu.VMEM((2, 2 * SIDE, 2 * SIDE), jnp.bfloat16),
            pltpu.VMEM((SIDE, SIDE), jnp.float32),
        ],
        compiler_params=pltpu.CompilerParams(vmem_limit_bytes=VMEM),
        cost_estimate=pl.CostEstimate(
            flops=16 * state.size * SIDE, bytes_accessed=8 * state.size, transcendentals=0
        ),
    )(pairs, masks, gates, state)


def middle_kernel(layer, pairs_ref, x_ref, gates_ref, in_ref, out_ref, stacks, table, first, second):
    @pl.when(pl.program_id(0) == 0)
    def _():
        stacks[0] = gate_stack(gates_ref[layer, 0])
        stacks[1] = gate_stack(gates_ref[layer, 1])
        rows = lax.broadcasted_iota(jnp.int32, (SIDE, SIDE), 0)
        lanes = lax.broadcasted_iota(jnp.int32, (SIDE, SIDE), 1)
        positions = x_ref[0] * (SIDE * SIDE) + lanes * SIDE + rows
        table[...] = sign_of(positions, pairs_ref, layer)

    stack_z = stacks[0]
    stack_y = stacks[1]

    def square(ref, b):
        return ref[:, b].reshape(SIDE, SIDE)

    for b in range(0, 16, 2):
        value = jnp.concatenate([square(in_ref, b), square(in_ref, b + 1)], 1)
        value = apply_rows(stack_y, value)
        first[b] = value[:, :SIDE].T.reshape(16, 8, SIDE)
        first[b + 1] = value[:, SIDE:].T.reshape(16, 8, SIDE)
    for d in range(0, 16, 2):
        value = jnp.concatenate([square(first, d), square(first, d + 1)], 1)
        value = apply_rows(stack_z, value)
        second[d] = (value[:, :SIDE] * table[...]).reshape(16, 8, SIDE)
        second[d + 1] = (value[:, SIDE:] * table[...]).reshape(16, 8, SIDE)
    for b in range(16):
        out_ref[:, b] = square(second, b).T.reshape(16, 8, SIDE)


def middle_layer(layer, pairs, x_index, gates, state):
    n_qa, n_qb, rows, _ = state.shape
    block = (n_qa, n_qb, 8, SIDE)
    return pl.pallas_call(
        functools.partial(middle_kernel, layer),
        grid=(rows // 8,),
        in_specs=[
            pl.BlockSpec(memory_space=pltpu.SMEM),
            pl.BlockSpec(memory_space=pltpu.SMEM),
            pl.BlockSpec(memory_space=pltpu.VMEM),
            pl.BlockSpec(block, lambda i: (0, 0, i, 0)),
        ],
        out_specs=pl.BlockSpec(block, lambda i: (0, 0, i, 0)),
        out_shape=jax.ShapeDtypeStruct(state.shape, jnp.float32),
        scratch_shapes=[
            pltpu.VMEM((2, 2 * SIDE, 2 * SIDE), jnp.bfloat16),
            pltpu.VMEM((SIDE, SIDE), jnp.float32),
            pltpu.VMEM((n_qb, 16, 8, SIDE), jnp.float32),
            pltpu.VMEM((16, n_qb, 8, SIDE), jnp.float32),
        ],
        compiler_params=pltpu.CompilerParams(vmem_limit_bytes=VMEM),
        cost_estimate=pl.CostEstimate(
            flops=16 * state.size * SIDE, bytes_accessed=8 * state.size, transcendentals=0
        ),
    )(pairs, x_index, gates, state)


def x_masks(pairs, count):
    x = jnp.arange(count, dtype=jnp.int32)[None]
    mask = jnp.zeros((2, count), jnp.int32)
    for pair in range(pairs.shape[1]):
        p = pairs[::2, pair, 0][:, None]
        q = pairs[::2, pair, 1][:, None]
        bit_p = jnp.where(p >= 14, jnp.right_shift(x, jnp.maximum(p - 14, 0)) & 1, 0)
        bit_q = jnp.where(q >= 14, jnp.right_shift(x, jnp.maximum(q - 14, 0)) & 1, 0)
        both = jnp.left_shift(bit_p & bit_q, 14)
        cross = jnp.where(
            q < 14,
            jnp.left_shift(bit_p, jnp.minimum(q, 14)),
            jnp.where(p < 14, jnp.left_shift(bit_q, jnp.minimum(p, 14)), both),
        )
        mask = mask ^ cross
    return mask


def per_device(amplitudes, gates, cz_pairs):
    total = amplitudes.shape[2]
    n_qa, n_qb = lax.axis_size("qa"), lax.axis_size("qb")
    state = amplitudes.reshape(total // SIDE, SIDE)
    masks = x_masks(cz_pairs, total // (SIDE * SIDE))
    device = lax.axis_index("qa") * n_qb + lax.axis_index("qb")
    x_index = jnp.right_shift(device, 2).astype(jnp.int32).reshape(1)
    blocks = n_qa * n_qb
    block_rows = total // SIDE // blocks
    state = native_layer(0, 0, cz_pairs, masks, gates, state)
    state = lax.all_to_all(state.reshape(blocks, block_rows, SIDE), AXES, 0, 0)
    state = state.reshape(n_qa, n_qb, block_rows, SIDE)
    state = middle_layer(1, cz_pairs, x_index, gates, state)
    state = lax.all_to_all(state.reshape(blocks, block_rows, SIDE), AXES, 0, 0)
    state = state.reshape(total // SIDE, SIDE)
    state = native_layer(2, 1, cz_pairs, masks, gates, state)
    return state.reshape(1, 1, total)


def solution(mesh):
    in_specs = (P("qa", "qb", None), P(), P())
    out_specs = P("qa", "qb", None)
    return jax.shard_map(
        per_device, mesh=mesh, in_specs=in_specs, out_specs=out_specs, check_vma=False
    )
```

```python
import functools

import jax
import jax.numpy as jnp
from jax import lax
from jax.experimental import pallas as pl
from jax.experimental.pallas import tpu as pltpu
from jax.sharding import PartitionSpec as P

LAYERS = 3
SIDE = 128
CHUNKS = 4
AXES = ("qa", "qb")
VMEM = 48 * 1024 * 1024


def split(value):
    high = value.astype(jnp.bfloat16)
    low = (value - high.astype(jnp.float32)).astype(jnp.bfloat16)
    return high, low


def gate_stack(gate):
    high, low = split(gate)
    high = jnp.concatenate([high, high], 1)
    low = jnp.concatenate([low, low], 1)
    rows = []
    for start in range(0, SIDE, 16):
        rows += [high[start : start + 16], low[start : start + 16]]
    return jnp.concatenate(rows, 0)


def gate_stack_lanes(gate):
    high, low = split(gate)
    return jnp.concatenate(
        [jnp.concatenate([high, high], 1), jnp.concatenate([low, low], 1)], 0
    )


def apply_rows(stack, value):
    high, low = split(value)
    both = jnp.dot(
        stack, jnp.concatenate([high, low], 0), preferred_element_type=jnp.float32
    )
    both = both.reshape(SIDE // 16, 2, 16, value.shape[1])
    return (both[:, 0] + both[:, 1]).reshape(value.shape)


def apply_lanes(stack, value):
    high, low = split(value)
    both = lax.dot_general(
        jnp.concatenate([high, low], 1),
        stack,
        (((1,), (1,)), ((), ())),
        preferred_element_type=jnp.float32,
    )
    return both[:, :SIDE] + both[:, SIDE:]


def sign_of(positions, pairs_ref, layer):
    parity = jnp.zeros(positions.shape, jnp.int32)
    for pair in range(pairs_ref.shape[2]):
        first = jnp.right_shift(positions, pairs_ref[layer, 0, pair])
        second = jnp.right_shift(positions, pairs_ref[layer, 1, pair])
        parity = parity ^ (first & second)
    return 1.0 - 2.0 * (parity & 1).astype(jnp.float32)


def fold_parity(value):
    for shift in (8, 4, 2, 1):
        value = value ^ jnp.right_shift(value, shift)
    return value & 1


def x_masks(x, pairs_ref, layer):
    x_bits = jnp.left_shift(x, 14)
    mask = jnp.zeros(x.shape, jnp.int32)
    for pair in range(pairs_ref.shape[2]):
        p = pairs_ref[layer, 0, pair]
        q = pairs_ref[layer, 1, pair]
        bit_p = jnp.right_shift(x_bits, p) & 1
        bit_q = jnp.right_shift(x_bits, q) & 1
        cross = jnp.left_shift(bit_p, q) ^ jnp.left_shift(bit_q, p)
        mask = mask ^ cross ^ jnp.left_shift(bit_p & bit_q, 20)
    return mask


def sign_table(x, layer, pairs_ref, y_first):
    first = lax.broadcasted_iota(jnp.int32, (SIDE, SIDE), 0)
    last = lax.broadcasted_iota(jnp.int32, (SIDE, SIDE), 1)
    y, z = (first, last) if y_first else (last, first)
    return sign_of(x * (SIDE * SIDE) + y * SIDE + z, pairs_ref, layer)


def native_pair(base, x, source, target, stack_z, stack_y, table, masks):
    low_bits = lax.broadcasted_iota(jnp.int32, (8, SIDE), 0) * SIDE + (
        lax.broadcasted_iota(jnp.int32, (8, SIDE), 1)
    )
    value = apply_lanes(stack_z[...], source[pl.ds(base, 2 * SIDE), :])
    value = apply_rows(stack_y[...], jnp.concatenate([value[:SIDE], value[SIDE:]], 1))
    for half in range(2):
        mask = jnp.broadcast_to(masks[pl.ds(x + half, 1), :], (8, SIDE))
        parity = fold_parity((low_bits & mask) ^ (jnp.right_shift(mask, 20) & 1))
        signs = [1.0 - 2.0 * parity.astype(jnp.float32)]
        for bit in range(4):
            flip = jnp.right_shift(mask, 10 + bit) & 1
            factor = 1.0 - 2.0 * flip.astype(jnp.float32)
            signs = signs + [sign * factor for sign in signs]
        sign = jnp.concatenate(signs, 0) * table[...]
        target[pl.ds(base + half * SIDE, SIDE), :] = (
            value[:, half * SIDE : (half + 1) * SIDE] * sign
        )


def first_kernel(
    pairs_ref, x_ref, gates_ref, in_ref, out_ref, stacks, tables, masks,
    gates, buffer, stack_z, stack_y, table, masks_0, gate_sem, sems,
):
    rows_chunk = in_ref.shape[0] // CHUNKS
    gate_copy = pltpu.make_async_copy(gates_ref, gates, gate_sem)
    gate_copy.start()

    def chunk_copy(chunk):
        part = pl.ds(chunk * rows_chunk, rows_chunk)
        return pltpu.make_async_copy(in_ref.at[part], buffer.at[part], sems.at[chunk])

    for chunk in range(CHUNKS):
        chunk_copy(chunk).start()

    table[...] = sign_table(0, 0, pairs_ref, True)
    tables[0] = sign_table(x_ref[0], 1, pairs_ref, False)
    tables[1] = sign_table(0, 2, pairs_ref, True)
    x = lax.broadcasted_iota(jnp.int32, masks.shape, 0)
    masks_0[...] = x_masks(x, pairs_ref, 0)
    masks[...] = x_masks(x, pairs_ref, 2)
    gate_copy.wait()
    stack_z[...] = gate_stack_lanes(gates[0, 0])
    stack_y[...] = gate_stack(gates[0, 1])
    stacks[0] = gate_stack(gates[1, 0])
    stacks[1] = gate_stack(gates[1, 1])
    stacks[2] = gate_stack_lanes(gates[2, 0])
    stacks[3] = gate_stack(gates[2, 1])

    for chunk in range(CHUNKS):
        chunk_copy(chunk).wait()
        for base in range(chunk * rows_chunk, (chunk + 1) * rows_chunk, 2 * SIDE):
            native_pair(
                base, base // SIDE, buffer, out_ref, stack_z, stack_y, table, masks_0
            )


def last_kernel(stacks, tables, masks, in_ref, out_ref, buffer, sems):
    rows_chunk = in_ref.shape[0] // CHUNKS

    def chunk_copy(chunk):
        part = pl.ds(chunk * rows_chunk, rows_chunk)
        return pltpu.make_async_copy(buffer.at[part], out_ref.at[part], sems.at[chunk])

    for chunk in range(CHUNKS):
        for base in range(chunk * rows_chunk, (chunk + 1) * rows_chunk, 2 * SIDE):
            native_pair(
                base, base // SIDE, in_ref, buffer,
                stacks.at[2], stacks.at[3], tables.at[1], masks,
            )
        chunk_copy(chunk).start()
    for chunk in range(CHUNKS):
        chunk_copy(chunk).wait()


def middle_kernel(stacks, tables, in_ref, out_ref, first, second):
    def square(ref, b, start):
        return ref[:, b, start : start + 8, :].reshape(SIDE, SIDE)

    for part in range(in_ref.shape[2] // 8):
        start = part * 8
        for b in range(0, 16, 2):
            value = jnp.concatenate(
                [square(in_ref, b, start), square(in_ref, b + 1, start)], 1
            )
            value = apply_rows(stacks[1], value)
            first[b] = value[:, :SIDE].T.reshape(16, 8, SIDE)
            first[b + 1] = value[:, SIDE:].T.reshape(16, 8, SIDE)
        for d in range(0, 16, 2):
            value = jnp.concatenate([square(first, d, 0), square(first, d + 1, 0)], 1)
            value = apply_rows(stacks[0], value)
            second[d] = (value[:, :SIDE] * tables[0]).reshape(16, 8, SIDE)
            second[d + 1] = (value[:, SIDE:] * tables[0]).reshape(16, 8, SIDE)
        for b in range(16):
            out_ref[:, b, start : start + 8, :] = square(second, b, 0).T.reshape(
                16, 8, SIDE
            )


WHOLE = pl.BlockSpec(memory_space=pltpu.VMEM)
SCALARS = pl.BlockSpec(memory_space=pltpu.SMEM)
REMOTE = pl.BlockSpec(memory_space=pl.ANY)


def call(kernel, state, in_specs, out_specs, out_shape, scratch_shapes):
    return pl.pallas_call(
        kernel,
        in_specs=in_specs,
        out_specs=out_specs,
        out_shape=out_shape,
        scratch_shapes=scratch_shapes,
        compiler_params=pltpu.CompilerParams(vmem_limit_bytes=VMEM),
        cost_estimate=pl.CostEstimate(
            flops=16 * state.size * SIDE, bytes_accessed=8 * state.size, transcendentals=0
        ),
    )


def first_layer(pairs, x_index, gates, state):
    n_x = state.shape[0] // SIDE
    stack = (2 * SIDE, 2 * SIDE)
    square = (SIDE, SIDE)
    return call(
        first_kernel,
        state,
        [SCALARS, SCALARS, REMOTE, REMOTE],
        [WHOLE] * 4,
        [
            jax.ShapeDtypeStruct(state.shape, jnp.float32),
            jax.ShapeDtypeStruct((4, *stack), jnp.bfloat16),
            jax.ShapeDtypeStruct((2, *square), jnp.float32),
            jax.ShapeDtypeStruct((n_x, SIDE), jnp.int32),
        ],
        [
            pltpu.VMEM(gates.shape, jnp.float32),
            pltpu.VMEM(state.shape, jnp.float32),
            pltpu.VMEM(stack, jnp.bfloat16),
            pltpu.VMEM(stack, jnp.bfloat16),
            pltpu.VMEM(square, jnp.float32),
            pltpu.VMEM((n_x, SIDE), jnp.int32),
            pltpu.SemaphoreType.DMA(()),
            pltpu.SemaphoreType.DMA((CHUNKS,)),
        ],
    )(pairs, x_index, gates, state)


def middle_layer(stacks, tables, state):
    return call(
        middle_kernel,
        state,
        [WHOLE] * 3,
        WHOLE,
        jax.ShapeDtypeStruct(state.shape, jnp.float32),
        [
            pltpu.VMEM((state.shape[1], 16, 8, SIDE), jnp.float32),
            pltpu.VMEM((16, state.shape[1], 8, SIDE), jnp.float32),
        ],
    )(stacks, tables, state)


def last_layer(stacks, tables, masks, state):
    return call(
        last_kernel,
        state,
        [WHOLE] * 4,
        REMOTE,
        jax.ShapeDtypeStruct(state.shape, jnp.float32),
        [
            pltpu.VMEM(state.shape, jnp.float32),
            pltpu.SemaphoreType.DMA((CHUNKS,)),
        ],
    )(stacks, tables, masks, state)


def per_device(amplitudes, gates, cz_pairs):
    total = amplitudes.shape[2]
    n_qa, n_qb = lax.axis_size("qa"), lax.axis_size("qb")
    pairs = cz_pairs.transpose(0, 2, 1)
    state = amplitudes.reshape(total // SIDE, SIDE)
    device = lax.axis_index("qa") * n_qb + lax.axis_index("qb")
    x_index = jnp.right_shift(device, 2).astype(jnp.int32).reshape(1)
    blocks = n_qa * n_qb
    block_rows = total // SIDE // blocks
    state, stacks, tables, masks = first_layer(pairs, x_index, gates, state)
    state = lax.all_to_all(state.reshape(blocks, block_rows, SIDE), AXES, 0, 0)
    state = state.reshape(n_qa, n_qb, block_rows, SIDE)
    state = middle_layer(stacks, tables, state)
    state = lax.all_to_all(state.reshape(blocks, block_rows, SIDE), AXES, 0, 0)
    state = state.reshape(total // SIDE, SIDE)
    state = last_layer(stacks, tables, masks, state)
    return state.reshape(1, 1, total)


def solution(mesh):
    in_specs = (P("qa", "qb", None), P(), P())
    out_specs = P("qa", "qb", None)
    return jax.shard_map(
        per_device, mesh=mesh, in_specs=in_specs, out_specs=out_specs, check_vma=False
    )
```

```python
import functools

import jax
import jax.numpy as jnp
from jax import lax
from jax.experimental import pallas as pl
from jax.experimental.pallas import tpu as pltpu
from jax.sharding import PartitionSpec as P

LAYERS = 3
SIDE = 128
IN_CHUNKS = 1
OUT_CHUNKS = 8
AXES = ("qa", "qb")
MIB = 1024 * 1024


def split(value):
    high = value.astype(jnp.bfloat16)
    low = (value - high.astype(jnp.float32)).astype(jnp.bfloat16)
    return high, low


def gate_stack(gate):
    high, low = split(gate)
    high = jnp.concatenate([high, high], 1)
    low = jnp.concatenate([low, low], 1)
    rows = []
    for start in range(0, SIDE, 16):
        rows += [high[start : start + 16], low[start : start + 16]]
    return jnp.concatenate(rows, 0)


def gate_stack_lanes(gate):
    high, low = split(gate)
    return jnp.concatenate(
        [jnp.concatenate([high, high], 1), jnp.concatenate([low, low], 1)], 0
    )


def apply_rows(stack, value):
    high, low = split(value)
    both = jnp.dot(
        stack, jnp.concatenate([high, low], 0), preferred_element_type=jnp.float32
    )
    both = both.reshape(SIDE // 16, 2, 16, value.shape[1])
    return (both[:, 0] + both[:, 1]).reshape(value.shape)


def apply_lanes(stack, value):
    high, low = split(value)
    both = lax.dot_general(
        jnp.concatenate([high, low], 1),
        stack,
        (((1,), (1,)), ((), ())),
        preferred_element_type=jnp.float32,
    )
    return both[:, :SIDE] + both[:, SIDE:]


def sign_of(positions, pairs_ref, layer):
    parity = jnp.zeros(positions.shape, jnp.int32)
    for pair in range(pairs_ref.shape[2]):
        first = jnp.right_shift(positions, pairs_ref[layer, 0, pair])
        second = jnp.right_shift(positions, pairs_ref[layer, 1, pair])
        parity = parity ^ (first & second)
    return 1.0 - 2.0 * (parity & 1).astype(jnp.float32)


def fold_parity(value):
    for shift in (8, 4, 2, 1):
        value = value ^ jnp.right_shift(value, shift)
    return value & 1


def x_masks(x, pairs_ref, layer):
    x_bits = jnp.left_shift(x, 14)
    mask = jnp.zeros(x.shape, jnp.int32)
    for pair in range(pairs_ref.shape[2]):
        p = pairs_ref[layer, 0, pair]
        q = pairs_ref[layer, 1, pair]
        bit_p = jnp.right_shift(x_bits, p) & 1
        bit_q = jnp.right_shift(x_bits, q) & 1
        cross = jnp.left_shift(bit_p, q) ^ jnp.left_shift(bit_q, p)
        mask = mask ^ cross ^ jnp.left_shift(bit_p & bit_q, 20)
    return mask


def sign_table(x, layer, pairs_ref, y_first):
    first = lax.broadcasted_iota(jnp.int32, (SIDE, SIDE), 0)
    last = lax.broadcasted_iota(jnp.int32, (SIDE, SIDE), 1)
    y, z = (first, last) if y_first else (last, first)
    return sign_of(x * (SIDE * SIDE) + y * SIDE + z, pairs_ref, layer)


def native_pair(base, x, source, target, stack_z, stack_y, table, masks):
    low_bits = lax.broadcasted_iota(jnp.int32, (8, SIDE), 0) * SIDE + (
        lax.broadcasted_iota(jnp.int32, (8, SIDE), 1)
    )
    value = apply_lanes(stack_z[...], source[pl.ds(base, 2 * SIDE), :])
    value = apply_rows(stack_y[...], jnp.concatenate([value[:SIDE], value[SIDE:]], 1))
    for half in range(2):
        mask = jnp.broadcast_to(masks[pl.ds(x + half, 1), :], (8, SIDE))
        parity = fold_parity((low_bits & mask) ^ (jnp.right_shift(mask, 20) & 1))
        signs = [1.0 - 2.0 * parity.astype(jnp.float32)]
        for bit in range(4):
            flip = jnp.right_shift(mask, 10 + bit) & 1
            factor = 1.0 - 2.0 * flip.astype(jnp.float32)
            signs = signs + [sign * factor for sign in signs]
        sign = jnp.concatenate(signs, 0) * table[...]
        target[pl.ds(base + half * SIDE, SIDE), :] = (
            value[:, half * SIDE : (half + 1) * SIDE] * sign
        )


def first_kernel(
    pairs_ref, x_ref, gates_ref, in_ref, out_ref, stacks, tables, masks,
    gates, buffer, stack_z, stack_y, table, masks_0, gate_sem, sems,
):
    rows_chunk = in_ref.shape[0] // IN_CHUNKS
    gate_copy = pltpu.make_async_copy(gates_ref, gates, gate_sem)
    gate_copy.start()

    def chunk_copy(chunk):
        part = pl.ds(chunk * rows_chunk, rows_chunk)
        return pltpu.make_async_copy(in_ref.at[part], buffer.at[part], sems.at[chunk])

    for chunk in range(IN_CHUNKS):
        chunk_copy(chunk).start()

    table[...] = sign_table(0, 0, pairs_ref, True)
    tables[0] = sign_table(x_ref[0], 1, pairs_ref, False)
    tables[1] = sign_table(0, 2, pairs_ref, True)
    x = lax.broadcasted_iota(jnp.int32, masks.shape, 0)
    masks_0[...] = x_masks(x, pairs_ref, 0)
    masks[...] = x_masks(x, pairs_ref, 2)
    gate_copy.wait()
    stack_z[...] = gate_stack_lanes(gates[0, 0])
    stack_y[...] = gate_stack(gates[0, 1])
    stacks[0] = gate_stack(gates[1, 0])
    stacks[1] = gate_stack(gates[1, 1])
    stacks[2] = gate_stack_lanes(gates[2, 0])
    stacks[3] = gate_stack(gates[2, 1])

    for chunk in range(IN_CHUNKS):
        chunk_copy(chunk).wait()
        for base in range(chunk * rows_chunk, (chunk + 1) * rows_chunk, 2 * SIDE):
            native_pair(
                base, base // SIDE, buffer, out_ref, stack_z, stack_y, table, masks_0
            )


def last_kernel(stacks, tables, masks, in_ref, out_ref, buffer, sems):
    rows_chunk = in_ref.shape[0] // OUT_CHUNKS

    def chunk_copy(chunk):
        part = pl.ds(chunk * rows_chunk, rows_chunk)
        return pltpu.make_async_copy(buffer.at[part], out_ref.at[part], sems.at[chunk])

    for chunk in range(OUT_CHUNKS):
        for base in range(chunk * rows_chunk, (chunk + 1) * rows_chunk, 2 * SIDE):
            native_pair(
                base, base // SIDE, in_ref, buffer,
                stacks.at[2], stacks.at[3], tables.at[1], masks,
            )
        chunk_copy(chunk).start()
    for chunk in range(OUT_CHUNKS):
        chunk_copy(chunk).wait()


def middle_kernel(stacks, tables, in_ref, out_ref, first, second):
    def square(ref, b, start):
        return ref[:, b, start : start + 8, :].reshape(SIDE, SIDE)

    for part in range(in_ref.shape[2] // 8):
        start = part * 8
        for b in range(0, 16, 2):
            value = jnp.concatenate(
                [square(in_ref, b, start), square(in_ref, b + 1, start)], 1
            )
            value = apply_rows(stacks[1], value)
            first[b] = value[:, :SIDE].T.reshape(16, 8, SIDE)
            first[b + 1] = value[:, SIDE:].T.reshape(16, 8, SIDE)
        for d in range(0, 16, 2):
            value = jnp.concatenate([square(first, d, 0), square(first, d + 1, 0)], 1)
            value = apply_rows(stacks[0], value)
            second[d] = (value[:, :SIDE] * tables[0]).reshape(16, 8, SIDE)
            second[d + 1] = (value[:, SIDE:] * tables[0]).reshape(16, 8, SIDE)
        for b in range(16):
            out_ref[:, b, start : start + 8, :] = square(second, b, 0).T.reshape(
                16, 8, SIDE
            )


WHOLE = pl.BlockSpec(memory_space=pltpu.VMEM)
SCALARS = pl.BlockSpec(memory_space=pltpu.SMEM)
REMOTE = pl.BlockSpec(memory_space=pl.ANY)


def call(kernel, state, in_specs, out_specs, out_shape, scratch_shapes, limit):
    return pl.pallas_call(
        kernel,
        in_specs=in_specs,
        out_specs=out_specs,
        out_shape=out_shape,
        scratch_shapes=scratch_shapes,
        compiler_params=pltpu.CompilerParams(vmem_limit_bytes=limit),
        cost_estimate=pl.CostEstimate(
            flops=16 * state.size * SIDE, bytes_accessed=8 * state.size, transcendentals=0
        ),
    )


def first_layer(pairs, x_index, gates, state):
    n_x = state.shape[0] // SIDE
    stack = (2 * SIDE, 2 * SIDE)
    square = (SIDE, SIDE)
    return call(
        first_kernel,
        state,
        [SCALARS, SCALARS, REMOTE, REMOTE],
        [WHOLE] * 4,
        [
            jax.ShapeDtypeStruct(state.shape, jnp.float32),
            jax.ShapeDtypeStruct((4, *stack), jnp.bfloat16),
            jax.ShapeDtypeStruct((2, *square), jnp.float32),
            jax.ShapeDtypeStruct((n_x, SIDE), jnp.int32),
        ],
        [
            pltpu.VMEM(gates.shape, jnp.float32),
            pltpu.VMEM(state.shape, jnp.float32),
            pltpu.VMEM(stack, jnp.bfloat16),
            pltpu.VMEM(stack, jnp.bfloat16),
            pltpu.VMEM(square, jnp.float32),
            pltpu.VMEM((n_x, SIDE), jnp.int32),
            pltpu.SemaphoreType.DMA(()),
            pltpu.SemaphoreType.DMA((IN_CHUNKS,)),
        ],
        48 * MIB,
    )(pairs, x_index, gates, state)


def middle_layer(stacks, tables, state):
    return call(
        middle_kernel,
        state,
        [WHOLE] * 3,
        WHOLE,
        jax.ShapeDtypeStruct(state.shape, jnp.float32),
        [
            pltpu.VMEM((state.shape[1], 16, 8, SIDE), jnp.float32),
            pltpu.VMEM((16, state.shape[1], 8, SIDE), jnp.float32),
        ],
        16 * MIB,
    )(stacks, tables, state)


def last_layer(stacks, tables, masks, state):
    return call(
        last_kernel,
        state,
        [WHOLE] * 4,
        REMOTE,
        jax.ShapeDtypeStruct(state.shape, jnp.float32),
        [
            pltpu.VMEM(state.shape, jnp.float32),
            pltpu.SemaphoreType.DMA((OUT_CHUNKS,)),
        ],
        16 * MIB,
    )(stacks, tables, masks, state)


def per_device(amplitudes, gates, cz_pairs):
    total = amplitudes.shape[2]
    n_qa, n_qb = lax.axis_size("qa"), lax.axis_size("qb")
    pairs = cz_pairs.transpose(0, 2, 1)
    state = amplitudes.reshape(total // SIDE, SIDE)
    device = lax.axis_index("qa") * n_qb + lax.axis_index("qb")
    x_index = jnp.right_shift(device, 2).astype(jnp.int32).reshape(1)
    blocks = n_qa * n_qb
    block_rows = total // SIDE // blocks
    state, stacks, tables, masks = first_layer(pairs, x_index, gates, state)
    state = lax.all_to_all(state.reshape(blocks, block_rows, SIDE), AXES, 0, 0)
    state = state.reshape(n_qa, n_qb, block_rows, SIDE)
    state = middle_layer(stacks, tables, state)
    state = lax.all_to_all(state.reshape(blocks, block_rows, SIDE), AXES, 0, 0)
    state = state.reshape(total // SIDE, SIDE)
    state = last_layer(stacks, tables, masks, state)
    return state.reshape(1, 1, total)


def solution(mesh):
    in_specs = (P("qa", "qb", None), P(), P())
    out_specs = P("qa", "qb", None)
    return jax.shard_map(
        per_device, mesh=mesh, in_specs=in_specs, out_specs=out_specs, check_vma=False
    )
```

```python
import functools

import jax
import jax.numpy as jnp
from jax import lax
from jax.experimental import pallas as pl
from jax.experimental.pallas import tpu as pltpu
from jax.sharding import PartitionSpec as P

LAYERS = 3
SIDE = 128
IN_CHUNKS = 2
OUT_CHUNKS = 8
GROUP = 1024
AXES = ("qa", "qb")
MIB = 1024 * 1024


def split(value):
    high = value.astype(jnp.bfloat16)
    low = (value - high.astype(jnp.float32)).astype(jnp.bfloat16)
    return high, low


def gate_stack(gate):
    high, low = split(gate)
    high = jnp.concatenate([high, high], 1)
    low = jnp.concatenate([low, low], 1)
    rows = []
    for start in range(0, SIDE, 16):
        rows += [high[start : start + 16], low[start : start + 16]]
    return jnp.concatenate(rows, 0)


def gate_stack_lanes(gate):
    high, low = split(gate)
    return jnp.concatenate(
        [jnp.concatenate([high, high], 1), jnp.concatenate([low, low], 1)], 0
    )


def apply_rows(stack, value):
    high, low = split(value)
    both = jnp.dot(
        stack, jnp.concatenate([high, low], 0), preferred_element_type=jnp.float32
    )
    both = both.reshape(SIDE // 16, 2, 16, value.shape[1])
    return (both[:, 0] + both[:, 1]).reshape(value.shape)


def apply_lanes(stack, value):
    high, low = split(value)
    both = lax.dot_general(
        jnp.concatenate([high, low], 1),
        stack,
        (((1,), (1,)), ((), ())),
        preferred_element_type=jnp.float32,
    )
    return both[:, :SIDE] + both[:, SIDE:]


def sign_of(positions, pairs_ref, layer):
    parity = jnp.zeros(positions.shape, jnp.int32)
    for pair in range(pairs_ref.shape[2]):
        first = jnp.right_shift(positions, pairs_ref[layer, 0, pair])
        second = jnp.right_shift(positions, pairs_ref[layer, 1, pair])
        parity = parity ^ (first & second)
    return 1.0 - 2.0 * (parity & 1).astype(jnp.float32)


def fold_parity(value):
    for shift in (8, 4, 2, 1):
        value = value ^ jnp.right_shift(value, shift)
    return value & 1


def x_masks(x, pairs_ref, layer):
    x_bits = jnp.left_shift(x, 14)
    mask = jnp.zeros(x.shape, jnp.int32)
    for pair in range(pairs_ref.shape[2]):
        p = pairs_ref[layer, 0, pair]
        q = pairs_ref[layer, 1, pair]
        bit_p = jnp.right_shift(x_bits, p) & 1
        bit_q = jnp.right_shift(x_bits, q) & 1
        cross = jnp.left_shift(bit_p, q) ^ jnp.left_shift(bit_q, p)
        mask = mask ^ cross ^ jnp.left_shift(bit_p & bit_q, 20)
    return mask


def sign_table(x, layer, pairs_ref, y_first):
    first = lax.broadcasted_iota(jnp.int32, (SIDE, SIDE), 0)
    last = lax.broadcasted_iota(jnp.int32, (SIDE, SIDE), 1)
    y, z = (first, last) if y_first else (last, first)
    return sign_of(x * (SIDE * SIDE) + y * SIDE + z, pairs_ref, layer)


def native_pair(base, x, value, target, stack_y, table, masks):
    low_bits = lax.broadcasted_iota(jnp.int32, (8, SIDE), 0) * SIDE + (
        lax.broadcasted_iota(jnp.int32, (8, SIDE), 1)
    )
    value = apply_rows(stack_y[...], jnp.concatenate([value[:SIDE], value[SIDE:]], 1))
    for half in range(2):
        mask = jnp.broadcast_to(masks[pl.ds(x + half, 1), :], (8, SIDE))
        parity = fold_parity((low_bits & mask) ^ (jnp.right_shift(mask, 20) & 1))
        signs = [1.0 - 2.0 * parity.astype(jnp.float32)]
        for bit in range(4):
            flip = jnp.right_shift(mask, 10 + bit) & 1
            factor = 1.0 - 2.0 * flip.astype(jnp.float32)
            signs = signs + [sign * factor for sign in signs]
        sign = jnp.concatenate(signs, 0) * table[...]
        target[pl.ds(base + half * SIDE, SIDE), :] = (
            value[:, half * SIDE : (half + 1) * SIDE] * sign
        )


def native_y(start, count, target, stack_y, table, masks):
    for base in range(start, start + count, 2 * SIDE):
        native_pair(
            base, base // SIDE, target[pl.ds(base, 2 * SIDE), :],
            target, stack_y, table, masks,
        )


def native_rows(start, count, source, target, stack_z, stack_y, table, masks):
    for group in range(start, start + count, GROUP):
        target[pl.ds(group, GROUP), :] = apply_lanes(stack_z[...], source[pl.ds(group, GROUP), :])
    for group in range(start, start + count, GROUP):
        for base in range(group, group + GROUP, 2 * SIDE):
            native_pair(
                base, base // SIDE, target[pl.ds(base, 2 * SIDE), :],
                target, stack_y, table, masks,
            )


def first_kernel(
    pairs_ref, x_ref, gates_ref, in_ref, out_ref, stacks, tables, masks,
    gates, buffer, stack_z, stack_y, table, masks_0, pairs, pair_sem, gate_sem, sems,
):
    pair_copy = pltpu.make_async_copy(pairs_ref, pairs, pair_sem)
    pair_copy.start()
    rows_chunk = in_ref.shape[0] // IN_CHUNKS
    gate_copy = pltpu.make_async_copy(gates_ref, gates, gate_sem)
    gate_copy.start()

    def chunk_copy(chunk):
        part = pl.ds(chunk * rows_chunk, rows_chunk)
        return pltpu.make_async_copy(in_ref.at[part], buffer.at[part], sems.at[chunk])

    for chunk in range(IN_CHUNKS):
        chunk_copy(chunk).start()

    pair_copy.wait()
    table[...] = sign_table(0, 0, pairs, True)
    tables[0] = sign_table(x_ref[0], 1, pairs, False)
    tables[1] = sign_table(0, 2, pairs, True)
    x = lax.broadcasted_iota(jnp.int32, masks.shape, 0)
    masks_0[...] = x_masks(x, pairs, 0)
    masks[...] = x_masks(x, pairs, 2)
    gate_copy.wait()
    stack_z[...] = gate_stack_lanes(gates[0, 0])
    stack_y[...] = gate_stack(gates[0, 1])
    stacks[0] = gate_stack(gates[1, 0])
    stacks[1] = gate_stack(gates[1, 1])
    stacks[2] = gate_stack_lanes(gates[2, 0])
    stacks[3] = gate_stack(gates[2, 1])

    for chunk in range(IN_CHUNKS):
        chunk_copy(chunk).wait()
        for group in range(chunk * rows_chunk, (chunk + 1) * rows_chunk, GROUP):
            part = pl.ds(group, GROUP)
            out_ref[part, :] = apply_lanes(stack_z[...], buffer[part, :])
    native_y(0, in_ref.shape[0], out_ref, stack_y, table, masks_0)


def last_kernel(stacks, tables, masks, in_ref, out_ref, buffer, sems):
    rows_chunk = in_ref.shape[0] // OUT_CHUNKS

    def chunk_copy(chunk):
        part = pl.ds(chunk * rows_chunk, rows_chunk)
        return pltpu.make_async_copy(buffer.at[part], out_ref.at[part], sems.at[chunk])

    for chunk in range(OUT_CHUNKS):
        native_rows(
            chunk * rows_chunk, rows_chunk, in_ref, buffer,
            stacks.at[2], stacks.at[3], tables.at[1], masks,
        )
        chunk_copy(chunk).start()
    for chunk in range(OUT_CHUNKS):
        chunk_copy(chunk).wait()


def middle_kernel(stacks, tables, in_ref, out_ref, first, second):
    def square(ref, b, start):
        return ref[:, b, start : start + 8, :].reshape(SIDE, SIDE)

    for part in range(in_ref.shape[2] // 8):
        start = part * 8
        for b in range(0, 16, 2):
            value = jnp.concatenate(
                [square(in_ref, b, start), square(in_ref, b + 1, start)], 1
            )
            value = apply_rows(stacks[1], value)
            first[b] = value[:, :SIDE].T.reshape(16, 8, SIDE)
            first[b + 1] = value[:, SIDE:].T.reshape(16, 8, SIDE)
        for d in range(0, 16, 2):
            value = jnp.concatenate([square(first, d, 0), square(first, d + 1, 0)], 1)
            value = apply_rows(stacks[0], value)
            second[d] = (value[:, :SIDE] * tables[0]).reshape(16, 8, SIDE)
            second[d + 1] = (value[:, SIDE:] * tables[0]).reshape(16, 8, SIDE)
        for b in range(16):
            out_ref[:, b, start : start + 8, :] = square(second, b, 0).T.reshape(
                16, 8, SIDE
            )


WHOLE = pl.BlockSpec(memory_space=pltpu.VMEM)
SCALARS = pl.BlockSpec(memory_space=pltpu.SMEM)
REMOTE = pl.BlockSpec(memory_space=pl.ANY)


def call(kernel, state, in_specs, out_specs, out_shape, scratch_shapes, limit):
    return pl.pallas_call(
        kernel,
        in_specs=in_specs,
        out_specs=out_specs,
        out_shape=out_shape,
        scratch_shapes=scratch_shapes,
        compiler_params=pltpu.CompilerParams(vmem_limit_bytes=limit),
        cost_estimate=pl.CostEstimate(
            flops=16 * state.size * SIDE, bytes_accessed=8 * state.size, transcendentals=0
        ),
    )


def in_hbm(value):
    return pltpu.with_memory_space_constraint(value, pltpu.HBM)


def first_layer(pairs, x_index, gates, state):
    n_x = state.shape[0] // SIDE
    stack = (2 * SIDE, 2 * SIDE)
    square = (SIDE, SIDE)
    return call(
        first_kernel,
        state,
        [REMOTE, SCALARS, REMOTE, REMOTE],
        [WHOLE] * 4,
        [
            jax.ShapeDtypeStruct(state.shape, jnp.float32),
            jax.ShapeDtypeStruct((4, *stack), jnp.bfloat16),
            jax.ShapeDtypeStruct((2, *square), jnp.float32),
            jax.ShapeDtypeStruct((n_x, SIDE), jnp.int32),
        ],
        [
            pltpu.VMEM(gates.shape, jnp.float32),
            pltpu.VMEM(state.shape, jnp.float32),
            pltpu.VMEM(stack, jnp.bfloat16),
            pltpu.VMEM(stack, jnp.bfloat16),
            pltpu.VMEM(square, jnp.float32),
            pltpu.VMEM((n_x, SIDE), jnp.int32),
            pltpu.SMEM(pairs.shape, jnp.int32),
            pltpu.SemaphoreType.DMA(()),
            pltpu.SemaphoreType.DMA(()),
            pltpu.SemaphoreType.DMA((IN_CHUNKS,)),
        ],
        48 * MIB,
    )(in_hbm(pairs), x_index, in_hbm(gates), state)


def middle_layer(stacks, tables, state):
    return call(
        middle_kernel,
        state,
        [WHOLE] * 3,
        WHOLE,
        jax.ShapeDtypeStruct(state.shape, jnp.float32),
        [
            pltpu.VMEM((state.shape[1], 16, 8, SIDE), jnp.float32),
            pltpu.VMEM((16, state.shape[1], 8, SIDE), jnp.float32),
        ],
        16 * MIB,
    )(stacks, tables, state)


def last_layer(stacks, tables, masks, state):
    return call(
        last_kernel,
        state,
        [WHOLE] * 4,
        REMOTE,
        jax.ShapeDtypeStruct(state.shape, jnp.float32),
        [
            pltpu.VMEM(state.shape, jnp.float32),
            pltpu.SemaphoreType.DMA((OUT_CHUNKS,)),
        ],
        16 * MIB,
    )(stacks, tables, masks, state)


def per_device(amplitudes, gates, cz_pairs):
    total = amplitudes.shape[2]
    n_qa, n_qb = lax.axis_size("qa"), lax.axis_size("qb")
    pairs = cz_pairs.transpose(0, 2, 1)
    state = amplitudes.reshape(total // SIDE, SIDE)
    device = lax.axis_index("qa") * n_qb + lax.axis_index("qb")
    x_index = jnp.right_shift(device, 2).astype(jnp.int32).reshape(1)
    blocks = n_qa * n_qb
    block_rows = total // SIDE // blocks
    state, stacks, tables, masks = first_layer(pairs, x_index, gates, state)
    state = lax.all_to_all(state.reshape(blocks, block_rows, SIDE), AXES, 0, 0)
    state = state.reshape(n_qa, n_qb, block_rows, SIDE)
    state = middle_layer(stacks, tables, state)
    state = lax.all_to_all(state.reshape(blocks, block_rows, SIDE), AXES, 0, 0)
    state = state.reshape(total // SIDE, SIDE)
    state = last_layer(stacks, tables, masks, state)
    return state.reshape(1, 1, total)


def solution(mesh):
    in_specs = (P("qa", "qb", None), P(), P())
    out_specs = P("qa", "qb", None)
    return jax.shard_map(
        per_device, mesh=mesh, in_specs=in_specs, out_specs=out_specs, check_vma=False
    )
```

```python
import functools

import jax
import jax.numpy as jnp
from jax import lax
from jax.experimental import pallas as pl
from jax.experimental.pallas import tpu as pltpu
from jax.sharding import PartitionSpec as P

SIDE = 128
IN_CHUNKS = 2
OUT_CHUNKS = 8
GROUP = 1024
AXES = ("qa", "qb")
MIB = 1024 * 1024


def split(value):
    high = value.astype(jnp.bfloat16)
    low = (value - high.astype(jnp.float32)).astype(jnp.bfloat16)
    return high, low


def gate_stack(gate):
    high, low = split(gate)
    high = jnp.concatenate([high, high], 1)
    low = jnp.concatenate([low, low], 1)
    rows = []
    for start in range(0, SIDE, 16):
        rows += [high[start : start + 16], low[start : start + 16]]
    return jnp.concatenate(rows, 0)


def gate_stack_lanes(gate):
    high, low = split(gate)
    return jnp.concatenate(
        [jnp.concatenate([high, high], 1), jnp.concatenate([low, low], 1)], 0
    )


def apply_rows(stack, value):
    high, low = split(value)
    both = jnp.dot(
        stack, jnp.concatenate([high, low], 0), preferred_element_type=jnp.float32
    )
    both = both.reshape(SIDE // 16, 2, 16, value.shape[1])
    return (both[:, 0] + both[:, 1]).reshape(value.shape)


def apply_lanes(stack, value):
    high, low = split(value)
    both = lax.dot_general(
        jnp.concatenate([high, low], 1),
        stack,
        (((1,), (1,)), ((), ())),
        preferred_element_type=jnp.float32,
    )
    return both[:, :SIDE] + both[:, SIDE:]


def sign_of(positions, pairs_ref, layer):
    parity = jnp.zeros(positions.shape, jnp.int32)
    for pair in range(pairs_ref.shape[2]):
        first = jnp.right_shift(positions, pairs_ref[layer, 0, pair])
        second = jnp.right_shift(positions, pairs_ref[layer, 1, pair])
        parity = parity ^ (first & second)
    return 1.0 - 2.0 * (parity & 1).astype(jnp.float32)


def fold_parity(value):
    for shift in (8, 4, 2, 1):
        value = value ^ jnp.right_shift(value, shift)
    return value & 1


def x_masks(x, pairs_ref, layer):
    x_bits = jnp.left_shift(x, 14)
    mask = jnp.zeros(x.shape, jnp.int32)
    for pair in range(pairs_ref.shape[2]):
        p = pairs_ref[layer, 0, pair]
        q = pairs_ref[layer, 1, pair]
        bit_p = jnp.right_shift(x_bits, p) & 1
        bit_q = jnp.right_shift(x_bits, q) & 1
        cross = jnp.left_shift(bit_p, q) ^ jnp.left_shift(bit_q, p)
        mask = mask ^ cross ^ jnp.left_shift(bit_p & bit_q, 20)
    return mask


def sign_table(x, layer, pairs_ref, y_first):
    first = lax.broadcasted_iota(jnp.int32, (SIDE, SIDE), 0)
    last = lax.broadcasted_iota(jnp.int32, (SIDE, SIDE), 1)
    y, z = (first, last) if y_first else (last, first)
    return sign_of(x * (SIDE * SIDE) + y * SIDE + z, pairs_ref, layer)


def native_pair(base, x, value, target, stack_y, table, masks):
    low_bits = lax.broadcasted_iota(jnp.int32, (8, SIDE), 0) * SIDE + (
        lax.broadcasted_iota(jnp.int32, (8, SIDE), 1)
    )
    value = apply_rows(stack_y[...], jnp.concatenate([value[:SIDE], value[SIDE:]], 1))
    for half in range(2):
        mask = jnp.broadcast_to(masks[pl.ds(x + half, 1), :], (8, SIDE))
        parity = fold_parity((low_bits & mask) ^ (jnp.right_shift(mask, 20) & 1))
        signs = [1.0 - 2.0 * parity.astype(jnp.float32)]
        for bit in range(4):
            flip = jnp.right_shift(mask, 10 + bit) & 1
            factor = 1.0 - 2.0 * flip.astype(jnp.float32)
            signs = signs + [sign * factor for sign in signs]
        sign = jnp.concatenate(signs, 0) * table[...]
        target[pl.ds(base + half * SIDE, SIDE), :] = (
            value[:, half * SIDE : (half + 1) * SIDE] * sign
        )


def native_y(start, count, target, stack_y, table, masks):
    for base in range(start, start + count, 2 * SIDE):
        native_pair(
            base, base // SIDE, target[pl.ds(base, 2 * SIDE), :],
            target, stack_y, table, masks,
        )


def first_kernel(
    pairs_ref, x_ref, gates_ref, in_ref, out_ref, stacks, tables, masks,
    gates, buffer, stack_z, stack_y, table, masks_0, pairs, pair_sem, gate_sem, sems,
):
    pair_copy = pltpu.make_async_copy(pairs_ref, pairs, pair_sem)
    pair_copy.start()
    rows_chunk = in_ref.shape[0] // IN_CHUNKS
    gate_copy = pltpu.make_async_copy(gates_ref, gates, gate_sem)
    gate_copy.start()

    def chunk_copy(chunk):
        part = pl.ds(chunk * rows_chunk, rows_chunk)
        return pltpu.make_async_copy(in_ref.at[part], buffer.at[part], sems.at[chunk])

    for chunk in range(IN_CHUNKS):
        chunk_copy(chunk).start()

    pair_copy.wait()
    table[...] = sign_table(0, 0, pairs, True)
    tables[0] = sign_table(x_ref[0], 1, pairs, False)
    tables[1] = sign_table(0, 2, pairs, True)
    x = lax.broadcasted_iota(jnp.int32, masks.shape, 0)
    masks_0[...] = x_masks(x, pairs, 0)
    masks[...] = x_masks(x, pairs, 2)
    gate_copy.wait()
    stack_z[...] = gate_stack_lanes(gates[0, 0])
    stack_y[...] = gate_stack(gates[0, 1])
    stacks[0] = gate_stack(gates[1, 0])
    stacks[1] = gate_stack(gates[1, 1])
    stacks[2] = gate_stack_lanes(gates[2, 0])
    stacks[3] = gate_stack(gates[2, 1])

    for chunk in range(IN_CHUNKS):
        chunk_copy(chunk).wait()
        for group in range(chunk * rows_chunk, (chunk + 1) * rows_chunk, GROUP):
            part = pl.ds(group, GROUP)
            out_ref[part, :] = apply_lanes(stack_z[...], buffer[part, :])
    native_y(0, in_ref.shape[0], out_ref, stack_y, table, masks_0)


def last_kernel(stacks, tables, masks, in_ref, out_ref, buffer, sems):
    rows_chunk = in_ref.shape[0] // OUT_CHUNKS

    def chunk_copy(chunk):
        part = pl.ds(chunk * rows_chunk, rows_chunk)
        return pltpu.make_async_copy(buffer.at[part], out_ref.at[part], sems.at[chunk])

    def gate_z(base):
        part = pl.ds(base, 2 * SIDE)
        buffer[part, :] = apply_lanes(stacks[2], in_ref[part, :])

    def gate_y(base):
        native_y(base, 2 * SIDE, buffer, stacks.at[3], tables.at[1], masks)

    for chunk in range(OUT_CHUNKS + 1):
        for base in range(chunk * rows_chunk, (chunk + 1) * rows_chunk, 2 * SIDE):
            if chunk < OUT_CHUNKS:
                gate_z(base)
            if chunk > 0:
                gate_y(base - rows_chunk)
        if chunk > 0:
            chunk_copy(chunk - 1).start()
    for chunk in range(OUT_CHUNKS):
        chunk_copy(chunk).wait()


def middle_kernel(stacks, tables, in_ref, out_ref, first, second):
    def square(ref, b, start):
        return ref[:, b, start : start + 8, :].reshape(SIDE, SIDE)

    parts = in_ref.shape[2] // 8

    def gate_y(part, b):
        value = jnp.concatenate(
            [square(in_ref, b, part * 8), square(in_ref, b + 1, part * 8)], 1
        )
        value = apply_rows(stacks[1], value)
        slot = first.at[part % 2]
        slot[b] = value[:, :SIDE].T.reshape(16, 8, SIDE)
        slot[b + 1] = value[:, SIDE:].T.reshape(16, 8, SIDE)

    def gate_z(part, d):
        source, target = first.at[part % 2], second.at[part % 2]
        value = jnp.concatenate([square(source, d, 0), square(source, d + 1, 0)], 1)
        value = apply_rows(stacks[0], value)
        target[d] = (value[:, :SIDE] * tables[0]).reshape(16, 8, SIDE)
        target[d + 1] = (value[:, SIDE:] * tables[0]).reshape(16, 8, SIDE)

    def turn(part, b):
        for one in (b, b + 1):
            value = square(second.at[part % 2], one, 0).T.reshape(16, 8, SIDE)
            out_ref[:, one, part * 8 : part * 8 + 8, :] = value

    for part in range(parts + 2):
        for b in range(0, 16, 2):
            if part < parts:
                gate_y(part, b)
            if 0 <= part - 1 < parts:
                gate_z(part - 1, b)
            if 0 <= part - 2 < parts:
                turn(part - 2, b)


WHOLE = pl.BlockSpec(memory_space=pltpu.VMEM)
SCALARS = pl.BlockSpec(memory_space=pltpu.SMEM)
REMOTE = pl.BlockSpec(memory_space=pl.ANY)


def call(kernel, state, in_specs, out_specs, out_shape, scratch_shapes, limit):
    return pl.pallas_call(
        kernel,
        in_specs=in_specs,
        out_specs=out_specs,
        out_shape=out_shape,
        scratch_shapes=scratch_shapes,
        compiler_params=pltpu.CompilerParams(vmem_limit_bytes=limit),
        cost_estimate=pl.CostEstimate(
            flops=16 * state.size * SIDE, bytes_accessed=8 * state.size, transcendentals=0
        ),
    )


def in_hbm(value):
    return pltpu.with_memory_space_constraint(value, pltpu.HBM)


def first_layer(pairs, x_index, gates, state):
    n_x = state.shape[0] // SIDE
    stack = (2 * SIDE, 2 * SIDE)
    square = (SIDE, SIDE)
    return call(
        first_kernel,
        state,
        [REMOTE, SCALARS, REMOTE, REMOTE],
        [WHOLE] * 4,
        [
            jax.ShapeDtypeStruct(state.shape, jnp.float32),
            jax.ShapeDtypeStruct((4, *stack), jnp.bfloat16),
            jax.ShapeDtypeStruct((2, *square), jnp.float32),
            jax.ShapeDtypeStruct((n_x, SIDE), jnp.int32),
        ],
        [
            pltpu.VMEM(gates.shape, jnp.float32),
            pltpu.VMEM(state.shape, jnp.float32),
            pltpu.VMEM(stack, jnp.bfloat16),
            pltpu.VMEM(stack, jnp.bfloat16),
            pltpu.VMEM(square, jnp.float32),
            pltpu.VMEM((n_x, SIDE), jnp.int32),
            pltpu.SMEM(pairs.shape, jnp.int32),
            pltpu.SemaphoreType.DMA(()),
            pltpu.SemaphoreType.DMA(()),
            pltpu.SemaphoreType.DMA((IN_CHUNKS,)),
        ],
        48 * MIB,
    )(in_hbm(pairs), x_index, in_hbm(gates), state)


def middle_layer(stacks, tables, state):
    return call(
        middle_kernel,
        state,
        [WHOLE] * 3,
        WHOLE,
        jax.ShapeDtypeStruct(state.shape, jnp.float32),
        [
            pltpu.VMEM((2, state.shape[1], 16, 8, SIDE), jnp.float32),
            pltpu.VMEM((2, 16, state.shape[1], 8, SIDE), jnp.float32),
        ],
        16 * MIB,
    )(stacks, tables, state)


def last_layer(stacks, tables, masks, state):
    return call(
        last_kernel,
        state,
        [WHOLE] * 4,
        REMOTE,
        jax.ShapeDtypeStruct(state.shape, jnp.float32),
        [
            pltpu.VMEM(state.shape, jnp.float32),
            pltpu.SemaphoreType.DMA((OUT_CHUNKS,)),
        ],
        16 * MIB,
    )(stacks, tables, masks, state)


def per_device(amplitudes, gates, cz_pairs):
    total = amplitudes.shape[2]
    n_qa, n_qb = lax.axis_size("qa"), lax.axis_size("qb")
    pairs = cz_pairs.transpose(0, 2, 1)
    state = amplitudes.reshape(total // SIDE, SIDE)
    device = lax.axis_index("qa") * n_qb + lax.axis_index("qb")
    x_index = jnp.right_shift(device, 2).astype(jnp.int32).reshape(1)
    blocks = n_qa * n_qb
    block_rows = total // SIDE // blocks
    state, stacks, tables, masks = first_layer(pairs, x_index, gates, state)
    state = lax.all_to_all(state.reshape(blocks, block_rows, SIDE), AXES, 0, 0)
    state = state.reshape(n_qa, n_qb, block_rows, SIDE)
    state = middle_layer(stacks, tables, state)
    state = lax.all_to_all(state.reshape(blocks, block_rows, SIDE), AXES, 0, 0)
    state = state.reshape(total // SIDE, SIDE)
    state = last_layer(stacks, tables, masks, state)
    return state.reshape(1, 1, total)


def solution(mesh):
    in_specs = (P("qa", "qb", None), P(), P())
    out_specs = P("qa", "qb", None)
    return jax.shard_map(
        per_device, mesh=mesh, in_specs=in_specs, out_specs=out_specs, check_vma=False
    )
```

```python
import functools

import jax
import jax.numpy as jnp
from jax import lax
from jax.experimental import pallas as pl
from jax.experimental.pallas import tpu as pltpu
from jax.sharding import PartitionSpec as P

SIDE = 128
IN_CHUNKS = 2
OUT_CHUNKS = 8
GROUP = 1024
TURNED_EVERY = 3
AXES = ("qa", "qb")
MIB = 1024 * 1024


def split(value):
    high = value.astype(jnp.bfloat16)
    low = (value - high.astype(jnp.float32)).astype(jnp.bfloat16)
    return high, low


def gate_stack(gate):
    high, low = split(gate)
    high = jnp.concatenate([high, high], 1)
    low = jnp.concatenate([low, low], 1)
    rows = []
    for start in range(0, SIDE, 16):
        rows += [high[start : start + 16], low[start : start + 16]]
    return jnp.concatenate(rows, 0)


def gate_stack_lanes(gate):
    high, low = split(gate)
    return jnp.concatenate(
        [jnp.concatenate([high, high], 1), jnp.concatenate([low, low], 1)], 0
    )


def apply_rows(stack, value):
    high, low = split(value)
    both = jnp.dot(
        stack, jnp.concatenate([high, low], 0), preferred_element_type=jnp.float32
    )
    both = both.reshape(SIDE // 16, 2, 16, value.shape[1])
    return (both[:, 0] + both[:, 1]).reshape(value.shape)


def apply_lanes(stack, value):
    high, low = split(value)
    both = lax.dot_general(
        jnp.concatenate([high, low], 1),
        stack,
        (((1,), (1,)), ((), ())),
        preferred_element_type=jnp.float32,
    )
    return both[:, :SIDE] + both[:, SIDE:]


def sign_of(positions, pairs_ref, layer):
    parity = jnp.zeros(positions.shape, jnp.int32)
    for pair in range(pairs_ref.shape[2]):
        first = jnp.right_shift(positions, pairs_ref[layer, 0, pair])
        second = jnp.right_shift(positions, pairs_ref[layer, 1, pair])
        parity = parity ^ (first & second)
    return 1.0 - 2.0 * (parity & 1).astype(jnp.float32)


def fold_parity(value):
    for shift in (8, 4, 2, 1):
        value = value ^ jnp.right_shift(value, shift)
    return value & 1


def x_masks(x, pairs_ref, layer):
    x_bits = jnp.left_shift(x, 14)
    mask = jnp.zeros(x.shape, jnp.int32)
    for pair in range(pairs_ref.shape[2]):
        p = pairs_ref[layer, 0, pair]
        q = pairs_ref[layer, 1, pair]
        bit_p = jnp.right_shift(x_bits, p) & 1
        bit_q = jnp.right_shift(x_bits, q) & 1
        cross = jnp.left_shift(bit_p, q) ^ jnp.left_shift(bit_q, p)
        mask = mask ^ cross ^ jnp.left_shift(bit_p & bit_q, 20)
    return mask


def sign_table(x, layer, pairs_ref, y_first):
    first = lax.broadcasted_iota(jnp.int32, (SIDE, SIDE), 0)
    last = lax.broadcasted_iota(jnp.int32, (SIDE, SIDE), 1)
    y, z = (first, last) if y_first else (last, first)
    return sign_of(x * (SIDE * SIDE) + y * SIDE + z, pairs_ref, layer)


def native_pair(base, x, value, target, stack_y, turned, table, masks):
    low_bits = lax.broadcasted_iota(jnp.int32, (8, SIDE), 0) * SIDE + (
        lax.broadcasted_iota(jnp.int32, (8, SIDE), 1)
    )
    if turned is None:
        value = jnp.concatenate([value[:SIDE], value[SIDE:]], 1)
        value = apply_rows(stack_y[...], value)
    else:
        value = jnp.concatenate([value[:SIDE].T, value[SIDE:].T], 0)
        value = apply_lanes(turned[...], value)
        value = jnp.concatenate([value[:SIDE].T, value[SIDE:].T], 1)
    for half in range(2):
        mask = jnp.broadcast_to(masks[pl.ds(x + half, 1), :], (8, SIDE))
        parity = fold_parity((low_bits & mask) ^ (jnp.right_shift(mask, 20) & 1))
        signs = [1.0 - 2.0 * parity.astype(jnp.float32)]
        for bit in range(4):
            flip = jnp.right_shift(mask, 10 + bit) & 1
            factor = 1.0 - 2.0 * flip.astype(jnp.float32)
            signs = signs + [sign * factor for sign in signs]
        sign = jnp.concatenate(signs, 0) * table[...]
        target[pl.ds(base + half * SIDE, SIDE), :] = (
            value[:, half * SIDE : (half + 1) * SIDE] * sign
        )


def native_y(start, count, target, stack_y, turned, every, table, masks):
    for base in range(start, start + count, 2 * SIDE):
        native_pair(
            base, base // SIDE, target[pl.ds(base, 2 * SIDE), :], target, stack_y,
            turned if base // (2 * SIDE) % every == every - 1 else None, table, masks,
        )


def first_kernel(
    pairs_ref, x_ref, gates_ref, in_ref, out_ref, stacks, tables, masks,
    gates, buffer, stack_z, stack_y, turned, table, masks_0, pairs, pair_sem, gate_sem, sems,
):
    pair_copy = pltpu.make_async_copy(pairs_ref, pairs, pair_sem)
    pair_copy.start()
    rows_chunk = in_ref.shape[0] // IN_CHUNKS
    gate_copy = pltpu.make_async_copy(gates_ref, gates, gate_sem)
    gate_copy.start()

    def chunk_copy(chunk):
        part = pl.ds(chunk * rows_chunk, rows_chunk)
        return pltpu.make_async_copy(in_ref.at[part], buffer.at[part], sems.at[chunk])

    for chunk in range(IN_CHUNKS):
        chunk_copy(chunk).start()

    pair_copy.wait()
    table[...] = sign_table(0, 0, pairs, True)
    tables[0] = sign_table(x_ref[0], 1, pairs, False)
    tables[1] = sign_table(0, 2, pairs, True)
    x = lax.broadcasted_iota(jnp.int32, masks.shape, 0)
    masks_0[...] = x_masks(x, pairs, 0)
    masks[...] = x_masks(x, pairs, 2)
    gate_copy.wait()
    stack_z[...] = gate_stack_lanes(gates[0, 0])
    stack_y[...] = gate_stack(gates[0, 1])
    turned[...] = gate_stack_lanes(gates[0, 1])
    stacks[0] = gate_stack(gates[1, 0])
    stacks[1] = gate_stack_lanes(gates[1, 1])
    stacks[2] = gate_stack_lanes(gates[2, 0])
    stacks[3] = gate_stack_lanes(gates[2, 1])

    for chunk in range(IN_CHUNKS):
        chunk_copy(chunk).wait()
        for group in range(chunk * rows_chunk, (chunk + 1) * rows_chunk, GROUP):
            part = pl.ds(group, GROUP)
            out_ref[part, :] = apply_lanes(stack_z[...], buffer[part, :])
    native_y(
        0, in_ref.shape[0], out_ref, stack_y, turned, TURNED_EVERY, table, masks_0
    )


def last_kernel(stacks, tables, masks, in_ref, out_ref, buffer, sems):
    rows_chunk = in_ref.shape[0] // OUT_CHUNKS

    def chunk_copy(chunk):
        part = pl.ds(chunk * rows_chunk, rows_chunk)
        return pltpu.make_async_copy(buffer.at[part], out_ref.at[part], sems.at[chunk])

    def gate_z(base):
        part = pl.ds(base, 2 * SIDE)
        buffer[part, :] = apply_lanes(stacks[2], in_ref[part, :])

    def gate_y(base):
        native_y(
            base, 2 * SIDE, buffer, None, stacks.at[3], 1,
            tables.at[1], masks,
        )

    for chunk in range(OUT_CHUNKS + 1):
        for base in range(chunk * rows_chunk, (chunk + 1) * rows_chunk, 2 * SIDE):
            if chunk < OUT_CHUNKS:
                gate_z(base)
            if chunk > 0:
                gate_y(base - rows_chunk)
        if chunk > 0:
            chunk_copy(chunk - 1).start()
    for chunk in range(OUT_CHUNKS):
        chunk_copy(chunk).wait()


def middle_kernel(stacks, tables, in_ref, out_ref, first, second):
    def square(ref, b, start):
        return ref[:, b, start : start + 8, :].reshape(SIDE, SIDE)

    parts = in_ref.shape[2] // 8

    def gate_y(part, b):
        slot = first.at[part % 2]
        value = jnp.concatenate(
            [square(in_ref, b, part * 8).T, square(in_ref, b + 1, part * 8).T], 0
        )
        value = apply_lanes(stacks[1], value)
        slot[b] = value[:SIDE].reshape(16, 8, SIDE)
        slot[b + 1] = value[SIDE:].reshape(16, 8, SIDE)

    def gate_z(part, d):
        source, target = first.at[part % 2], second.at[part % 2]
        value = jnp.concatenate([square(source, d, 0), square(source, d + 1, 0)], 1)
        value = apply_rows(stacks[0], value)
        target[d] = (value[:, :SIDE] * tables[0]).reshape(16, 8, SIDE)
        target[d + 1] = (value[:, SIDE:] * tables[0]).reshape(16, 8, SIDE)

    def turn(part, b):
        for one in (b, b + 1):
            value = square(second.at[part % 2], one, 0).T.reshape(16, 8, SIDE)
            out_ref[:, one, part * 8 : part * 8 + 8, :] = value

    for part in range(parts + 2):
        for b in range(0, 16, 2):
            if part < parts:
                gate_y(part, b)
            if 0 <= part - 1 < parts:
                gate_z(part - 1, b)
            if 0 <= part - 2 < parts:
                turn(part - 2, b)


WHOLE = pl.BlockSpec(memory_space=pltpu.VMEM)
SCALARS = pl.BlockSpec(memory_space=pltpu.SMEM)
REMOTE = pl.BlockSpec(memory_space=pl.ANY)


def call(kernel, state, in_specs, out_specs, out_shape, scratch_shapes, limit):
    return pl.pallas_call(
        kernel,
        in_specs=in_specs,
        out_specs=out_specs,
        out_shape=out_shape,
        scratch_shapes=scratch_shapes,
        compiler_params=pltpu.CompilerParams(vmem_limit_bytes=limit),
        cost_estimate=pl.CostEstimate(
            flops=16 * state.size * SIDE, bytes_accessed=8 * state.size, transcendentals=0
        ),
    )


def in_hbm(value):
    return pltpu.with_memory_space_constraint(value, pltpu.HBM)


def first_layer(pairs, x_index, gates, state):
    n_x = state.shape[0] // SIDE
    stack = (2 * SIDE, 2 * SIDE)
    square = (SIDE, SIDE)
    return call(
        first_kernel,
        state,
        [REMOTE, SCALARS, REMOTE, REMOTE],
        [WHOLE] * 4,
        [
            jax.ShapeDtypeStruct(state.shape, jnp.float32),
            jax.ShapeDtypeStruct((4, *stack), jnp.bfloat16),
            jax.ShapeDtypeStruct((2, *square), jnp.float32),
            jax.ShapeDtypeStruct((n_x, SIDE), jnp.int32),
        ],
        [
            pltpu.VMEM(gates.shape, jnp.float32),
            pltpu.VMEM(state.shape, jnp.float32),
            pltpu.VMEM(stack, jnp.bfloat16),
            pltpu.VMEM(stack, jnp.bfloat16),
            pltpu.VMEM(stack, jnp.bfloat16),
            pltpu.VMEM(square, jnp.float32),
            pltpu.VMEM((n_x, SIDE), jnp.int32),
            pltpu.SMEM(pairs.shape, jnp.int32),
            pltpu.SemaphoreType.DMA(()),
            pltpu.SemaphoreType.DMA(()),
            pltpu.SemaphoreType.DMA((IN_CHUNKS,)),
        ],
        48 * MIB,
    )(in_hbm(pairs), x_index, in_hbm(gates), state)


def middle_layer(stacks, tables, state):
    return call(
        middle_kernel,
        state,
        [WHOLE] * 3,
        WHOLE,
        jax.ShapeDtypeStruct(state.shape, jnp.float32),
        [
            pltpu.VMEM((2, state.shape[1], 16, 8, SIDE), jnp.float32),
            pltpu.VMEM((2, 16, state.shape[1], 8, SIDE), jnp.float32),
        ],
        16 * MIB,
    )(stacks, tables, state)


def last_layer(stacks, tables, masks, state):
    return call(
        last_kernel,
        state,
        [WHOLE] * 4,
        REMOTE,
        jax.ShapeDtypeStruct(state.shape, jnp.float32),
        [
            pltpu.VMEM(state.shape, jnp.float32),
            pltpu.SemaphoreType.DMA((OUT_CHUNKS,)),
        ],
        16 * MIB,
    )(stacks, tables, masks, state)


def per_device(amplitudes, gates, cz_pairs):
    total = amplitudes.shape[2]
    n_qa, n_qb = lax.axis_size("qa"), lax.axis_size("qb")
    pairs = cz_pairs.transpose(0, 2, 1)
    state = amplitudes.reshape(total // SIDE, SIDE)
    device = lax.axis_index("qa") * n_qb + lax.axis_index("qb")
    x_index = jnp.right_shift(device, 2).astype(jnp.int32).reshape(1)
    blocks = n_qa * n_qb
    block_rows = total // SIDE // blocks
    state, stacks, tables, masks = first_layer(pairs, x_index, gates, state)
    state = lax.all_to_all(state.reshape(blocks, block_rows, SIDE), AXES, 0, 0)
    state = state.reshape(n_qa, n_qb, block_rows, SIDE)
    state = middle_layer(stacks, tables, state)
    state = lax.all_to_all(state.reshape(blocks, block_rows, SIDE), AXES, 0, 0)
    state = state.reshape(total // SIDE, SIDE)
    state = last_layer(stacks, tables, masks, state)
    return state.reshape(1, 1, total)


def solution(mesh):
    in_specs = (P("qa", "qb", None), P(), P())
    out_specs = P("qa", "qb", None)
    return jax.shard_map(
        per_device, mesh=mesh, in_specs=in_specs, out_specs=out_specs, check_vma=False
    )
```
